32 devices in a mesh: vp: 16 (over z, y, x), red: 2 (over core).
Axes of the slice: x: 2, y: 2, z: 4, core: 2. Of those that a mesh axis runs over, the one named last changes fastest.
Arguments:
- t2_amps: bfloat16 [256, 32768], P('vp', 'red'), may hold values from -6 to 6
- integrals: bfloat16 [32768, 1024], P(('red', 'vp')), may hold values from -0.1875 to 0.1875
- ij_irrep: int32 [256], replicated, may hold values from 0 to 7, as said below
- cd_irrep: int32 [32768], P(('red', 'vp')), may hold values from 0 to 7, as said below
- ab_irrep: int32 [1024], replicated, may hold values from 0 to 7, as said below
Outputs:
- ladder: float32 [256, 1024], P('vp', 'red')
The draws below stay inside these ranges and needn't reach their ends.
Inputs may be any that keep to these rules, and one draw needn't show every extreme that they name: Most occupied pairs carry one irrep, drawn from the seed and the same for ij_irrep, cd_irrep and ab_irrep; the other pairs are spread over the remaining seven irreps. `cd_irrep`: most contracted pairs carry the common irrep of the three label arrays; the others are spread over the remaining seven irreps. `ab_irrep`: most pairs of the slab carry the common irrep of the three label arrays; the others are spread over the remaining seven irreps.
All inputs are finite; a program needn't handle non-finite values.
Results may differ from the reference program's by a relative error of at most 0.0003.
Values may be sent and summed in bfloat16 or wider, within the bound.
A program may use at most 64 MiB of HBM per device.

```python
import jax
import jax.numpy as jnp
from jax import lax

CD_DEV = 1024
AB = 1024
IJ = 256
CD = 32768


def common_irrep(key):
    return jax.random.randint(jax.random.fold_in(key, 7), (), 0, 8)


def skewed_labels(key, count, rarity, salt):
    base = common_irrep(key)
    mixed = jax.random.fold_in(key, salt)
    first_key, second_key = jax.random.split(mixed)
    picked = jax.random.randint(first_key, (count,), 0, rarity)
    offset = jax.random.randint(second_key, (count,), 1, 8)
    return jnp.where(picked == 0, jnp.bitwise_xor(base, offset), base).astype(jnp.int32)


def draw_ij_irrep(key, part):
    return skewed_labels(key, IJ, 8, 11)


def draw_cd_irrep(key, part):
    return skewed_labels(key, CD, 8, 13)


def draw_ab_irrep(key, part):
    return skewed_labels(key, AB, 16, 17)


def raised(drawn, key, source, target, parts, factor):
    owner, partner = [(jnp.arange(drawn.shape[position]) // (drawn.shape[position] // parts)).reshape([-1 if axis == position else 1 for axis in range(drawn.ndim)]) for position in (source, target)]
    chosen = jax.random.permutation(key, parts)[partner]
    strong = (owner == chosen) | (owner == (partner + parts // 2) % parts)
    return jnp.where(strong, factor * drawn, drawn)


def level_of(rng, dims, shards, smallest, largest):
    gain, own = 1.0, jax.random.fold_in(rng, 6)
    for axis_at, parts in shards:
        draws = jnp.exp(jax.random.uniform(jax.random.fold_in(own, axis_at), (parts,), jnp.float32, smallest / len(shards), largest / len(shards)))
        gain = gain * jnp.repeat(draws, dims[axis_at] // parts).reshape([-1 if axis == axis_at else 1 for axis in range(len(dims))])
    return gain


def scatter_about(rng, extent, deviation, most, shards=(), kind=jnp.bfloat16):
    array = jax.random.normal(rng, extent, jnp.float32) * deviation
    if len(shards) > 0:
        array = level_of(rng, extent, shards, -0.22, 0.18) * array
    return jnp.clip(array, min=-most, max=most).astype(kind)


def noise_with(stream_key, shape, deviation, bound, pieces, heavy, kind=jnp.bfloat16):
    drawn = deviation * jax.random.normal(stream_key, shape, jnp.float32)
    if pieces:
        drawn = drawn * level_of(stream_key, shape, pieces, -0.22, 0.18)
    return jnp.clip(raised(drawn, jax.random.fold_in(stream_key, 3), *heavy), -bound, bound).astype(kind)


def setup_inputs(seed: int = 0) -> dict:
    keys = jax.random.split(jax.random.key(seed), 6)
    return {
        "t2_amps": scatter_about(keys[0], (IJ, CD), 1.0, 6.0, ((0, 16), (1, 2))),
        "integrals": noise_with(keys[1], (CD, AB), (CD // 8) ** -0.5, 0.1875, ((0, 32),), (0, 1, 32, 2.75)),
        "ij_irrep": draw_ij_irrep(jax.random.fold_in(keys[5], 71), 0),
        "cd_irrep": draw_cd_irrep(jax.random.fold_in(keys[5], 71), 0),
        "ab_irrep": draw_ab_irrep(jax.random.fold_in(keys[5], 71), 0),
    }


def reference(t2_amps, integrals, ij_irrep, cd_irrep, ab_irrep):
    block = CD_DEV
    count = CD // block
    zero_t = jnp.zeros((), t2_amps.dtype)
    zero_v = jnp.zeros((), integrals.dtype)

    def step(index, total):
        start = (index * block).astype(jnp.int32)
        t_piece = lax.dynamic_slice_in_dim(t2_amps, start, block, 1)
        v_piece = lax.dynamic_slice_in_dim(integrals, start, block, 0)
        labels = lax.dynamic_slice_in_dim(cd_irrep, start, block, 0)
        t_sym = jnp.where(ij_irrep[:, None] == labels[None, :], t_piece, zero_t)
        v_sym = jnp.where(labels[:, None] == ab_irrep[None, :], v_piece, zero_v)
        return total + jnp.dot(t_sym, v_sym, preferred_element_type=jnp.float32)

    start_total = jnp.zeros((t2_amps.shape[0], integrals.shape[1]), jnp.float32)
    return lax.fori_loop(0, count, step, start_total)
```

```python
import functools
import math

import jax
import jax.numpy as jnp
from jax import lax
from jax.experimental import pallas as pl
from jax.experimental.pallas import tpu as pltpu
from jax.sharding import PartitionSpec as P

MESH = pl.DeviceIdType.MESH


def group_of(n):
    size = math.isqrt(n)
    while n % size:
        size -= 1
    return size


def order_of(planes):
    return sorted(range(planes), key=lambda d: (min(d, planes - d), d))


def kernel(
    n, r, size, t_ref, v_ref, ij_hbm, cd_hbm, ab_hbm, out_ref,
    ij_ref, cd_ref, ab_ref, tbuf, vbuf, labels, part, redbuf, own, planebuf, comb, zbuf,
    load_sem, t_send, t_recv, r_send, r_recv, p_send, p_recv, z_send, z_recv,
):
    planes = n // size
    me, core = lax.axis_index("vp"), lax.axis_index("red")
    plane, place = lax.div(me, size), lax.rem(me, size)
    rows, depth = tbuf.shape[1], tbuf.shape[2]
    width = out_ref.shape[1]
    order = order_of(planes)

    def block(who):
        return t_ref.at[:, pl.ds(pl.multiple_of(who * depth, depth), depth)]

    load_v = pltpu.make_async_copy(v_ref, vbuf, load_sem.at[0])
    load_t = pltpu.make_async_copy(block(me), tbuf.at[me], load_sem.at[1])
    load_labels = [
        pltpu.make_async_copy(src, dst, load_sem.at[2 + i])
        for i, (src, dst) in enumerate(
            [(ij_hbm, ij_ref), (cd_hbm, cd_ref), (ab_hbm, ab_ref)]
        )
    ]
    for copy in (load_t, *load_labels, load_v):
        copy.start()

    barrier = pltpu.get_barrier_semaphore()
    for d in range(1, n):
        pl.semaphore_signal(
            barrier, inc=1, device_id=(lax.rem(me + d, n), core), device_id_type=MESH
        )
    for d in range(1, r):
        pl.semaphore_signal(
            barrier, inc=1, device_id=(me, lax.rem(core + d, r)), device_id_type=MESH
        )
    pl.semaphore_wait(barrier, n - 1 + r - 1)

    t_copies = {}
    for dz in order:
        for dp in range(size):
            if dz == 0 and dp == 0:
                continue
            who = lax.rem(plane + dz, planes) * size + lax.rem(place + dp, size)
            copy = pltpu.make_async_remote_copy(
                src_ref=block(who),
                dst_ref=tbuf.at[me],
                send_sem=t_send.at[dz, dp],
                recv_sem=t_recv.at[dz, dp],
                device_id=(who, core),
                device_id_type=MESH,
            )
            copy.start()
            t_copies[dz, dp] = copy

    for copy in load_labels:
        copy.wait()
    labels[...] = jnp.transpose(jnp.broadcast_to(ij_ref[...], (128, ij_ref.shape[1])))
    load_t.wait()
    load_v.wait()

    sent = []

    def multiply(step):
        dz = order[step]
        for dp in range(size):
            if (dz, dp) in t_copies:
                t_copies[dz, dp].wait_recv()
        source = lax.rem(plane + planes - dz, planes)
        amps = tbuf[pl.ds(source * size, size)].reshape(size * rows, depth)
        first = pl.multiple_of(source * (size * rows), size * rows)
        kept = labels[pl.ds(first, size * rows), :][:, :1] == cd_ref[...]
        amps = jnp.where(kept, amps.astype(jnp.float32), 0.0).astype(amps.dtype)
        copies = []
        for d in [*range(1, r), 0]:
            to = lax.rem(core + d, r)
            columns = pl.ds(pl.multiple_of(to * width, width), width)
            part[step, d] = jnp.dot(
                amps, vbuf[:, columns], preferred_element_type=jnp.float32
            )
            if d:
                copy = pltpu.make_async_remote_copy(
                    src_ref=part.at[step, d],
                    dst_ref=redbuf.at[step, d - 1],
                    send_sem=r_send.at[step, d - 1],
                    recv_sem=r_recv.at[step, d - 1],
                    device_id=(me, to),
                    device_id_type=MESH,
                )
                copy.start()
                copies.append(copy)
                sent.append(copy)
        return copies

    def spread(step, copies):
        total = part[step, 0]
        for d, copy in enumerate(copies):
            copy.wait_recv()
            total = total + redbuf[step, d]
        own[step] = total.reshape(size, rows, width)
        out = []
        for d in range(1, size):
            to = lax.rem(place + d, size)
            copy = pltpu.make_async_remote_copy(
                src_ref=own.at[step, to],
                dst_ref=planebuf.at[step, d - 1],
                send_sem=p_send.at[step, d - 1],
                recv_sem=p_recv.at[step, d - 1],
                device_id=(plane * size + to, core),
                device_id_type=MESH,
            )
            copy.start()
            out.append(copy)
            sent.append(copy)
        return out

    def gather(step, copies):
        total = own[step, place]
        for d, copy in enumerate(copies):
            copy.wait_recv()
            total = total + planebuf[step, d]
        comb[step] = total
        if step == 0:
            return None
        owner = lax.rem(plane + planes - order[step], planes)
        copy = pltpu.make_async_remote_copy(
            src_ref=comb.at[step],
            dst_ref=zbuf.at[step - 1],
            send_sem=z_send.at[step - 1],
            recv_sem=z_recv.at[step - 1],
            device_id=(owner * size + place, core),
            device_id_type=MESH,
        )
        copy.start()
        sent.append(copy)
        return copy

    last, finals = None, []
    for step in range(planes):
        copies = multiply(step)
        if last is not None:
            finals.append(gather(step - 1, last))
        last = spread(step, copies)
    finals.append(gather(planes - 1, last))

    total = comb[0]
    for step in range(1, planes):
        finals[step].wait_recv()
        total = total + zbuf[step - 1]
    mine = labels[pl.ds(pl.multiple_of(me * rows, rows), rows), :][:, :1]
    theirs = ab_ref[:, pl.ds(pl.multiple_of(core * width, width), width)]
    out_ref[...] = jnp.where(mine == theirs, total, 0.0)

    for copy in [*t_copies.values(), *sent]:
        copy.wait_send()


def shards(n, r, t2_amps, integrals, ij_irrep, cd_irrep, ab_irrep):
    rows = t2_amps.shape[0]
    depth, wide = integrals.shape
    width = wide // r
    size = group_of(n)
    planes = n // size
    f32 = jnp.float32
    dma = pltpu.SemaphoreType.DMA
    vmem = pl.BlockSpec(memory_space=pltpu.VMEM)
    hbm = pl.BlockSpec(memory_space=pltpu.HBM)
    return pl.pallas_call(
        functools.partial(kernel, n, r, size),
        out_shape=jax.ShapeDtypeStruct((rows, width), f32),
        in_specs=[hbm] * 5,
        out_specs=vmem,
        scratch_shapes=[
            pltpu.VMEM((1, n * rows), jnp.int32),
            pltpu.VMEM((1, depth), jnp.int32),
            pltpu.VMEM((1, wide), jnp.int32),
            pltpu.VMEM((n, rows, depth), t2_amps.dtype),
            pltpu.VMEM((depth, wide), integrals.dtype),
            pltpu.VMEM((n * rows, 128), jnp.int32),
            pltpu.VMEM((planes, r, size * rows, width), f32),
            pltpu.VMEM((planes, max(r - 1, 1), size * rows, width), f32),
            pltpu.VMEM((planes, size, rows, width), f32),
            pltpu.VMEM((planes, max(size - 1, 1), rows, width), f32),
            pltpu.VMEM((planes, rows, width), f32),
            pltpu.VMEM((max(planes - 1, 1), rows, width), f32),
            dma((5,)),
            dma((planes, size)),
            dma((planes, size)),
            dma((planes, max(r - 1, 1))),
            dma((planes, max(r - 1, 1))),
            dma((planes, max(size - 1, 1))),
            dma((planes, max(size - 1, 1))),
            dma((max(planes - 1, 1),)),
            dma((max(planes - 1, 1),)),
        ],
        cost_estimate=pl.CostEstimate(
            flops=2 * n * rows * depth * wide,
            bytes_accessed=2 * (n * rows * depth + depth * wide) + 4 * rows * width,
            transcendentals=0,
        ),
        compiler_params=pltpu.CompilerParams(
            collective_id=0, has_side_effects=True, vmem_limit_bytes=60 * 2**20
        ),
    )(t2_amps, integrals, ij_irrep[None, :], cd_irrep[None, :], ab_irrep[None, :])


def solution(mesh):
    placed = (P("vp", "red"), P(("red", "vp"), None), P(), P(("red", "vp")), P())
    return jax.shard_map(
        functools.partial(shards, mesh.shape["vp"], mesh.shape["red"]),
        mesh=mesh,
        in_specs=placed,
        out_specs=P("vp", "red"),
        check_vma=False,
    )
```

```python
import functools
import math

import jax
import jax.numpy as jnp
from jax import lax
from jax.experimental import pallas as pl
from jax.experimental.pallas import tpu as pltpu
from jax.sharding import PartitionSpec as P

MESH = pl.DeviceIdType.MESH


def group_of(n):
    size = math.isqrt(n)
    while n % size:
        size -= 1
    return size


def order_of(planes):
    return [0, *sorted(range(1, planes), key=lambda d: (-min(d, planes - d), -d))]


def kernel(
    n, r, size, t_ref, v_ref, ij_hbm, cd_hbm, ab_hbm, out_ref,
    ij_ref, cd_ref, ab_ref, tbuf, vbuf, labels, part, redbuf, own, planebuf, comb, zbuf,
    load_sem, t_send, t_recv, r_send, r_recv, p_send, p_recv, z_send, z_recv,
):
    planes = n // size
    me, core = lax.axis_index("vp"), lax.axis_index("red")
    plane, place = lax.div(me, size), lax.rem(me, size)
    rows, depth = tbuf.shape[1], tbuf.shape[2]
    width = out_ref.shape[1]
    order = order_of(planes)

    def block(who):
        return t_ref.at[:, pl.ds(pl.multiple_of(who * depth, depth), depth)]

    load_v = pltpu.make_async_copy(v_ref, vbuf, load_sem.at[0])
    load_t = pltpu.make_async_copy(block(me), tbuf.at[me], load_sem.at[1])
    load_labels = [
        pltpu.make_async_copy(src, dst, load_sem.at[2 + i])
        for i, (src, dst) in enumerate(
            [(ij_hbm, ij_ref), (cd_hbm, cd_ref), (ab_hbm, ab_ref)]
        )
    ]
    for copy in (load_t, *load_labels, load_v):
        copy.start()

    barrier = pltpu.get_barrier_semaphore()
    for d in range(1, n):
        pl.semaphore_signal(
            barrier, inc=1, device_id=(lax.rem(me + d, n), core), device_id_type=MESH
        )
    for d in range(1, r):
        pl.semaphore_signal(
            barrier, inc=1, device_id=(me, lax.rem(core + d, r)), device_id_type=MESH
        )
    pl.semaphore_wait(barrier, n - 1 + r - 1)

    t_copies = {}
    for dz in order:
        for dp in range(size):
            if dz == 0 and dp == 0:
                continue
            who = lax.rem(plane + dz, planes) * size + lax.rem(place + dp, size)
            copy = pltpu.make_async_remote_copy(
                src_ref=block(who),
                dst_ref=tbuf.at[me],
                send_sem=t_send.at[dz, dp],
                recv_sem=t_recv.at[dz, dp],
                device_id=(who, core),
                device_id_type=MESH,
            )
            copy.start()
            t_copies[dz, dp] = copy

    for copy in load_labels:
        copy.wait()
    labels[...] = jnp.transpose(jnp.broadcast_to(ij_ref[...], (128, ij_ref.shape[1])))
    load_t.wait()
    load_v.wait()

    sent = []

    def multiply(step):
        dz = order[step]
        for dp in range(size):
            if (dz, dp) in t_copies:
                t_copies[dz, dp].wait_recv()
        source = lax.rem(plane + planes - dz, planes)
        amps = tbuf[pl.ds(source * size, size)].reshape(size * rows, depth)
        first = pl.multiple_of(source * (size * rows), size * rows)
        kept = labels[pl.ds(first, size * rows), :][:, :1] == cd_ref[...]
        amps = jnp.where(kept, amps.astype(jnp.float32), 0.0).astype(amps.dtype)
        copies = []
        for d in [*range(1, r), 0]:
            to = lax.rem(core + d, r)
            columns = pl.ds(pl.multiple_of(to * width, width), width)
            part[step, d] = jnp.dot(
                amps, vbuf[:, columns], preferred_element_type=jnp.float32
            )
            if d:
                copy = pltpu.make_async_remote_copy(
                    src_ref=part.at[step, d],
                    dst_ref=redbuf.at[step, d - 1],
                    send_sem=r_send.at[step, d - 1],
                    recv_sem=r_recv.at[step, d - 1],
                    device_id=(me, to),
                    device_id_type=MESH,
                )
                copy.start()
                copies.append(copy)
                sent.append(copy)
        return copies

    def spread(step, copies):
        total = part[step, 0]
        for d, copy in enumerate(copies):
            copy.wait_recv()
            total = total + redbuf[step, d]
        own[step] = total.reshape(size, rows, width)
        out = []
        for d in range(1, size):
            to = lax.rem(place + d, size)
            copy = pltpu.make_async_remote_copy(
                src_ref=own.at[step, to],
                dst_ref=planebuf.at[step, d - 1],
                send_sem=p_send.at[step, d - 1],
                recv_sem=p_recv.at[step, d - 1],
                device_id=(plane * size + to, core),
                device_id_type=MESH,
            )
            copy.start()
            out.append(copy)
            sent.append(copy)
        return out

    def gather(step, copies):
        total = own[step, place]
        for d, copy in enumerate(copies):
            copy.wait_recv()
            total = total + planebuf[step, d]
        comb[step] = total
        dz = order[step]
        if dz == 0:
            return None
        owner = lax.rem(plane + planes - dz, planes)
        copy = pltpu.make_async_remote_copy(
            src_ref=comb.at[step],
            dst_ref=zbuf.at[dz - 1],
            send_sem=z_send.at[dz - 1],
            recv_sem=z_recv.at[dz - 1],
            device_id=(owner * size + place, core),
            device_id_type=MESH,
        )
        copy.start()
        sent.append(copy)
        return copy

    last, finals = None, []
    for step in range(planes):
        copies = multiply(step)
        if last is not None:
            finals.append(gather(step - 1, last))
        last = spread(step, copies)
    finals.append(gather(planes - 1, last))

    total = comb[order.index(0)]
    for step, dz in enumerate(order):
        if dz:
            finals[step].wait_recv()
            total = total + zbuf[dz - 1]
    mine = labels[pl.ds(pl.multiple_of(me * rows, rows), rows), :][:, :1]
    theirs = ab_ref[:, pl.ds(pl.multiple_of(core * width, width), width)]
    out_ref[...] = jnp.where(mine == theirs, total, 0.0)

    for copy in [*t_copies.values(), *sent]:
        copy.wait_send()


def shards(n, r, t2_amps, integrals, ij_irrep, cd_irrep, ab_irrep):
    rows = t2_amps.shape[0]
    depth, wide = integrals.shape
    width = wide // r
    size = group_of(n)
    planes = n // size
    f32 = jnp.float32
    dma = pltpu.SemaphoreType.DMA
    vmem = pl.BlockSpec(memory_space=pltpu.VMEM)
    hbm = pl.BlockSpec(memory_space=pltpu.HBM)
    return pl.pallas_call(
        functools.partial(kernel, n, r, size),
        out_shape=jax.ShapeDtypeStruct((rows, width), f32),
        in_specs=[hbm] * 5,
        out_specs=vmem,
        scratch_shapes=[
            pltpu.VMEM((1, n * rows), jnp.int32),
            pltpu.VMEM((1, depth), jnp.int32),
            pltpu.VMEM((1, wide), jnp.int32),
            pltpu.VMEM((n, rows, depth), t2_amps.dtype),
            pltpu.VMEM((depth, wide), integrals.dtype),
            pltpu.VMEM((n * rows, 128), jnp.int32),
            pltpu.VMEM((planes, r, size * rows, width), f32),
            pltpu.VMEM((planes, max(r - 1, 1), size * rows, width), f32),
            pltpu.VMEM((planes, size, rows, width), f32),
            pltpu.VMEM((planes, max(size - 1, 1), rows, width), f32),
            pltpu.VMEM((planes, rows, width), f32),
            pltpu.VMEM((max(planes - 1, 1), rows, width), f32),
            dma((5,)),
            dma((planes, size)),
            dma((planes, size)),
            dma((planes, max(r - 1, 1))),
            dma((planes, max(r - 1, 1))),
            dma((planes, max(size - 1, 1))),
            dma((planes, max(size - 1, 1))),
            dma((max(planes - 1, 1),)),
            dma((max(planes - 1, 1),)),
        ],
        cost_estimate=pl.CostEstimate(
            flops=2 * n * rows * depth * wide,
            bytes_accessed=2 * (n * rows * depth + depth * wide) + 4 * rows * width,
            transcendentals=0,
        ),
        compiler_params=pltpu.CompilerParams(
            collective_id=0, has_side_effects=True, vmem_limit_bytes=60 * 2**20
        ),
    )(t2_amps, integrals, ij_irrep[None, :], cd_irrep[None, :], ab_irrep[None, :])


def solution(mesh):
    placed = (P("vp", "red"), P(("red", "vp"), None), P(), P(("red", "vp")), P())
    return jax.shard_map(
        functools.partial(shards, mesh.shape["vp"], mesh.shape["red"]),
        mesh=mesh,
        in_specs=placed,
        out_specs=P("vp", "red"),
        check_vma=False,
    )
```

```python
import functools
import math

import jax
import jax.numpy as jnp
from jax import lax
from jax.experimental import pallas as pl
from jax.experimental.pallas import tpu as pltpu
from jax.sharding import PartitionSpec as P

MESH = pl.DeviceIdType.MESH


def group_of(n):
    size = math.isqrt(n)
    while n % size:
        size -= 1
    return size


def order_of(planes):
    return [0, *sorted(range(1, planes), key=lambda d: (-min(d, planes - d), -d))]


def kernel(
    n, r, size, t_ref, v_ref, ij_hbm, cd_hbm, ab_hbm, out_ref,
    ij_ref, cd_ref, ab_ref, tbuf, vbuf, labels, part, redbuf, own, planebuf, comb, zbuf,
    load_sem, t_send, t_recv, r_send, r_recv, p_send, p_recv, z_send, z_recv,
):
    planes = n // size
    me, core = lax.axis_index("vp"), lax.axis_index("red")
    plane, place = lax.div(me, size), lax.rem(me, size)
    rows, depth = tbuf.shape[1], tbuf.shape[2]
    width = out_ref.shape[1]
    order = order_of(planes)

    def block(who):
        return t_ref.at[:, pl.ds(pl.multiple_of(who * depth, depth), depth)]

    load_v = pltpu.make_async_copy(v_ref, vbuf, load_sem.at[0])
    load_t = pltpu.make_async_copy(block(me), tbuf.at[me], load_sem.at[1])
    load_labels = [
        pltpu.make_async_copy(src, dst, load_sem.at[2 + i])
        for i, (src, dst) in enumerate(
            [(ij_hbm, ij_ref), (cd_hbm, cd_ref), (ab_hbm, ab_ref)]
        )
    ]
    for copy in (load_t, *load_labels, load_v):
        copy.start()

    barrier = pltpu.get_barrier_semaphore()
    for d in range(1, n):
        pl.semaphore_signal(
            barrier, inc=1, device_id=(lax.rem(me + d, n), core), device_id_type=MESH
        )
    for d in range(1, r):
        pl.semaphore_signal(
            barrier, inc=1, device_id=(me, lax.rem(core + d, r)), device_id_type=MESH
        )
    pl.semaphore_wait(barrier, n - 1 + r - 1)

    t_copies = {}
    for dz in order:
        for dp in range(size):
            if dz == 0 and dp == 0:
                continue
            who = lax.rem(plane + dz, planes) * size + lax.rem(place + dp, size)
            copy = pltpu.make_async_remote_copy(
                src_ref=block(who),
                dst_ref=tbuf.at[me],
                send_sem=t_send.at[dz, dp],
                recv_sem=t_recv.at[dz, dp],
                device_id=(who, core),
                device_id_type=MESH,
            )
            copy.start()
            t_copies[dz, dp] = copy

    for copy in load_labels:
        copy.wait()
    labels[...] = jnp.transpose(jnp.broadcast_to(ij_ref[...], (128, ij_ref.shape[1])))
    load_t.wait()
    load_v.wait()

    sent = []

    def multiply(step):
        dz = order[step]
        for dp in range(size):
            if (dz, dp) in t_copies:
                t_copies[dz, dp].wait_recv()
        source = lax.rem(plane + planes - dz, planes)
        amps = tbuf[pl.ds(source * size, size)].reshape(size * rows, depth)
        first = pl.multiple_of(source * (size * rows), size * rows)
        kept = labels[pl.ds(first, size * rows), :][:, :1] == cd_ref[...]
        amps = jnp.where(kept, amps.astype(jnp.float32), 0.0).astype(amps.dtype)
        copies = []
        for d in [*range(1, r), 0]:
            to = lax.rem(core + d, r)
            columns = pl.ds(pl.multiple_of(to * width, width), width)
            part[step, d] = jnp.dot(
                amps, vbuf[:, columns], preferred_element_type=jnp.float32
            )
            if d:
                copy = pltpu.make_async_remote_copy(
                    src_ref=part.at[step, d],
                    dst_ref=redbuf.at[step, d - 1],
                    send_sem=r_send.at[step, d - 1],
                    recv_sem=r_recv.at[step, d - 1],
                    device_id=(me, to),
                    device_id_type=MESH,
                )
                copy.start()
                copies.append(copy)
                sent.append(copy)
        return copies

    def spread(step, copies):
        total = part[step, 0]
        for d, copy in enumerate(copies):
            copy.wait_recv()
            total = total + redbuf[step, d]
        own[step] = total.reshape(size, rows, width)
        out = []
        for d in range(1, size):
            to = lax.rem(place + d, size)
            copy = pltpu.make_async_remote_copy(
                src_ref=own.at[step, to],
                dst_ref=planebuf.at[step, d - 1],
                send_sem=p_send.at[step, d - 1],
                recv_sem=p_recv.at[step, d - 1],
                device_id=(plane * size + to, core),
                device_id_type=MESH,
            )
            copy.start()
            out.append(copy)
            sent.append(copy)
        return out

    def gather(step, copies):
        total = own[step, place]
        for d, copy in enumerate(copies):
            copy.wait_recv()
            total = total + planebuf[step, d]
        comb[step] = total
        dz = order[step]
        if dz == 0:
            return None
        owner = lax.rem(plane + planes - dz, planes)
        copy = pltpu.make_async_remote_copy(
            src_ref=comb.at[step],
            dst_ref=zbuf.at[dz - 1],
            send_sem=z_send.at[dz - 1],
            recv_sem=z_recv.at[dz - 1],
            device_id=(owner * size + place, core),
            device_id_type=MESH,
        )
        copy.start()
        sent.append(copy)
        return copy

    last, finals = None, []
    for step in range(planes):
        here = spread(step, multiply(step))
        if last is not None:
            finals.append(gather(step - 1, last))
        last = here
    finals.append(gather(planes - 1, last))

    total = comb[order.index(0)]
    for step, dz in enumerate(order):
        if dz:
            finals[step].wait_recv()
            total = total + zbuf[dz - 1]
    mine = labels[pl.ds(pl.multiple_of(me * rows, rows), rows), :][:, :1]
    theirs = ab_ref[:, pl.ds(pl.multiple_of(core * width, width), width)]
    out_ref[...] = jnp.where(mine == theirs, total, 0.0)

    for copy in [*t_copies.values(), *sent]:
        copy.wait_send()


def shards(n, r, t2_amps, integrals, ij_irrep, cd_irrep, ab_irrep):
    rows = t2_amps.shape[0]
    depth, wide = integrals.shape
    width = wide // r
    size = group_of(n)
    planes = n // size
    f32 = jnp.float32
    dma = pltpu.SemaphoreType.DMA
    vmem = pl.BlockSpec(memory_space=pltpu.VMEM)
    hbm = pl.BlockSpec(memory_space=pltpu.HBM)
    return pl.pallas_call(
        functools.partial(kernel, n, r, size),
        out_shape=jax.ShapeDtypeStruct((rows, width), f32),
        in_specs=[hbm] * 5,
        out_specs=vmem,
        scratch_shapes=[
            pltpu.VMEM((1, n * rows), jnp.int32),
            pltpu.VMEM((1, depth), jnp.int32),
            pltpu.VMEM((1, wide), jnp.int32),
            pltpu.VMEM((n, rows, depth), t2_amps.dtype),
            pltpu.VMEM((depth, wide), integrals.dtype),
            pltpu.VMEM((n * rows, 128), jnp.int32),
            pltpu.VMEM((planes, r, size * rows, width), f32),
            pltpu.VMEM((planes, max(r - 1, 1), size * rows, width), f32),
            pltpu.VMEM((planes, size, rows, width), f32),
            pltpu.VMEM((planes, max(size - 1, 1), rows, width), f32),
            pltpu.VMEM((planes, rows, width), f32),
            pltpu.VMEM((max(planes - 1, 1), rows, width), f32),
            dma((5,)),
            dma((planes, size)),
            dma((planes, size)),
            dma((planes, max(r - 1, 1))),
            dma((planes, max(r - 1, 1))),
            dma((planes, max(size - 1, 1))),
            dma((planes, max(size - 1, 1))),
            dma((max(planes - 1, 1),)),
            dma((max(planes - 1, 1),)),
        ],
        cost_estimate=pl.CostEstimate(
            flops=2 * n * rows * depth * wide,
            bytes_accessed=2 * (n * rows * depth + depth * wide) + 4 * rows * width,
            transcendentals=0,
        ),
        compiler_params=pltpu.CompilerParams(
            collective_id=0, has_side_effects=True, vmem_limit_bytes=60 * 2**20
        ),
    )(t2_amps, integrals, ij_irrep[None, :], cd_irrep[None, :], ab_irrep[None, :])


def solution(mesh):
    placed = (P("vp", "red"), P(("red", "vp"), None), P(), P(("red", "vp")), P())
    return jax.shard_map(
        functools.partial(shards, mesh.shape["vp"], mesh.shape["red"]),
        mesh=mesh,
        in_specs=placed,
        out_specs=P("vp", "red"),
        check_vma=False,
    )
```
